32 devices in a mesh: island: 8 (over y, x, core), fsdp: 4 (over z).
Axes of the slice: x: 2, y: 2, z: 4, core: 2. Of those that a mesh axis runs over, the one named last changes fastest.
Arguments:
- tokens: bfloat16 [8, 1024, 12288], P('island', 'fsdp'), may hold values from -6 to 6
- targets: bfloat16 [8, 1024, 256], P('island', 'fsdp'), may hold values from -6 to 6
- loss_mask: int32 [8, 1024], P('island', 'fsdp'), may hold values 0 or 1
- norm_gain: float32 [12288], replicated, may hold values from 0.5 to 1.5
- params: float32 [8, 12288, 256], P('island', 'fsdp'), may hold values from -0.0546875 to 0.0546875
- moment_one: float32 [8, 12288, 256], P('island', 'fsdp'), may hold values from -0.12 to 0.12
- moment_two: float32 [8, 12288, 256], P('island', 'fsdp'), may hold values from 0.0001 to 0.002
- outer_delta: float32 [8, 12288, 128], P('island', 'fsdp'), may hold values from -6 to 6
- outer_momentum: float32 [12288, 128], P('fsdp'), may hold values from -6 to 6
Outputs:
- params_new: float32 [8, 12288, 256], P('island', 'fsdp')
- momentum_new: float32 [12288, 128], P('fsdp')
- outer_update: float32 [12288, 128], P('fsdp')
The draws below stay inside these ranges and needn't reach their ends.
All inputs are finite; a program needn't handle non-finite values. No bound on the sum of `loss_mask` on one device may be relied on, other than what follows from the above.
Results may differ from the reference program's by a relative error of at most 0.0025.
Values may be sent and summed in bfloat16 or wider, within the bound.
A program may use at most 128 MiB of HBM per device.

```python
import math
import jax
import jax.numpy as jnp
from jax import lax

D = 12288
HD = 256
OHD = 128
TOK_ISL = 1024
ISLANDS = 8


def set_ends(array, rng, smallest, top_value):
    shape = array.shape
    place = [jax.random.randint(jax.random.fold_in(rng, axis), (), 0, shape[axis]) for axis in range(len(shape))]
    array = array.at[tuple(place)].set(smallest)
    longest = shape.index(max(shape))
    place[longest] = (place[longest] + 1) % shape[longest]
    return array.at[tuple(place)].set(top_value)


def level_of(key, dims, split, smallest, largest):
    level = 1.0
    for axis_at, blocks in split:
        draws = jax.random.uniform(jax.random.fold_in(jax.random.fold_in(key, 6), axis_at), (blocks,), jnp.float32, smallest / len(split), largest / len(split))
        level = level * jnp.repeat(jnp.exp(draws), dims[axis_at] // blocks).reshape((-1,) + (1,) * (len(dims) - 1 - axis_at))
    return level


def normal_values(rng, dims, spread, bound, shards=(), held_as=jnp.bfloat16):
    values = spread * jax.random.normal(rng, dims, jnp.float32)
    if shards:
        values = values * level_of(rng, dims, shards, -0.22, 0.18)
    return jnp.clip(values, -bound, bound).astype(held_as)


def setup_inputs(seed: int = 0) -> dict:
    arg_keys = jax.random.split(jax.random.key(seed), 10)
    tokens = normal_values(arg_keys[0], (ISLANDS, TOK_ISL, D), 1.0, 6.0, ((0, 8), (1, 4)))
    targets = normal_values(arg_keys[1], (ISLANDS, TOK_ISL, HD), 1.0, 6.0, ((0, 8), (1, 4)))
    loss_mask = set_ends((jax.random.randint(arg_keys[2], (ISLANDS, TOK_ISL), 0, 4) < 3).astype(jnp.int32), jax.random.fold_in(arg_keys[2], 1), 0, 1)
    norm_gain = jnp.clip(1.0 + 0.1 * jax.random.normal(arg_keys[3], (D,), jnp.float32), 0.5, 1.5)
    params = normal_values(arg_keys[4], (ISLANDS, D, HD), D ** -0.5, 0.0546875, ((0, 8), (1, 4)), jnp.float32)
    moment_one = normal_values(arg_keys[5], (ISLANDS, D, HD), 0.02, 0.12, ((0, 8), (1, 4)), jnp.float32)
    moment_two = jnp.clip(jnp.exp(math.log(0.002) - 2.9957323 * jax.random.uniform(arg_keys[6], (ISLANDS, D, HD), jnp.float32) ** level_of(arg_keys[6], (ISLANDS, D, HD), ((0, 8), (1, 4)), -0.2, 0.2)), 0.0001, 0.002)
    outer_delta = normal_values(arg_keys[7], (ISLANDS, D, OHD), 1.0, 6.0, ((0, 8), (1, 4)), jnp.float32)
    outer_momentum = normal_values(arg_keys[8], (D, OHD), 1.0, 6.0, ((0, 4),), jnp.float32)
    return {"tokens": tokens, "targets": targets, "loss_mask": loss_mask, "norm_gain": norm_gain, "params": params, "moment_one": moment_one, "moment_two": moment_two, "outer_delta": outer_delta, "outer_momentum": outer_momentum}


ADAM_BETA_ONE = 0.9
ADAM_BETA_TWO = 0.95
ADAM_EPSILON = 1e-08
INNER_RATE = 0.005
WEIGHT_DECAY = 0.1
NORM_EPSILON = 1e-05
OUTER_RATE = 0.7
OUTER_MOMENTUM = 0.9
STEP_BASE = 1000

def adam_update(weights, first_moment, second_moment, gradient, count):
    first_moment = ADAM_BETA_ONE * first_moment + (1.0 - ADAM_BETA_ONE) * gradient
    second_moment = ADAM_BETA_TWO * second_moment + (1.0 - ADAM_BETA_TWO) * gradient * gradient
    first_hat = first_moment / (1.0 - ADAM_BETA_ONE ** count)
    second_hat = second_moment / (1.0 - ADAM_BETA_TWO ** count)
    weights = weights - INNER_RATE * (first_hat / (jnp.sqrt(second_hat) + ADAM_EPSILON) + WEIGHT_DECAY * weights)
    return (weights, first_moment, second_moment)

def reference(tokens, targets, loss_mask, norm_gain, params, moment_one, moment_two, outer_delta, outer_momentum):

    def one_island(pieces):
        rows_in, goal_in, mask_in, weights, first_moment, second_moment = pieces
        inputs_f = rows_in.astype(jnp.float32)
        row_scale = lax.rsqrt(lax.optimization_barrier(jnp.mean(inputs_f * inputs_f, axis=1)) + NORM_EPSILON)
        scaled = (inputs_f * norm_gain).astype(jnp.bfloat16)
        keep_rows = mask_in.astype(jnp.float32)
        goal_rows = goal_in.astype(jnp.float32)
        token_count = scaled.shape[0]
        for inner_step in range(2):
            weights_bf = weights.astype(jnp.bfloat16)
            value_rows = row_scale[:, None] * jnp.dot(scaled, weights_bf, preferred_element_type=jnp.float32)
            residual_rows = (row_scale[:, None] * keep_rows[:, None] * (value_rows - goal_rows) / token_count).astype(jnp.bfloat16)
            gradient = lax.dot_general(scaled, residual_rows, (((0,), (0,)), ((), ())), preferred_element_type=jnp.float32)
            weights, first_moment, second_moment = adam_update(weights, first_moment, second_moment, gradient, float(STEP_BASE + inner_step + 1))
        return weights
    params_new = lax.map(one_island, (tokens, targets, loss_mask, params, moment_one, moment_two))
    outer_mean = lax.optimization_barrier(jnp.sum(outer_delta, axis=0)) / outer_delta.shape[0]
    momentum_new = OUTER_MOMENTUM * outer_momentum + outer_mean
    outer_update = OUTER_RATE * (outer_mean + OUTER_MOMENTUM * momentum_new)
    return (params_new, momentum_new, outer_update)
```

```python
import functools
import jax
import jax.numpy as jnp
from jax import lax
from jax.experimental import pallas as pl
from jax.experimental.pallas import tpu as pltpu
from jax.sharding import PartitionSpec as P

ADAM_BETA_ONE = 0.9
ADAM_BETA_TWO = 0.95
ADAM_EPSILON = 1e-08
INNER_RATE = 0.005
WEIGHT_DECAY = 0.1
NORM_EPSILON = 1e-05
OUTER_RATE = 0.7
OUTER_MOMENTUM = 0.9
STEP_BASE = 1000
MESH = pl.DeviceIdType.MESH
CHUNK = 128
BLOCK = 256


def adam_update(weights, first_moment, second_moment, gradient, count):
    first_moment = ADAM_BETA_ONE * first_moment + (1.0 - ADAM_BETA_ONE) * gradient
    second_moment = ADAM_BETA_TWO * second_moment + (1.0 - ADAM_BETA_TWO) * gradient * gradient
    first_hat = first_moment * (1.0 / (1.0 - ADAM_BETA_ONE**count))
    second_hat = second_moment * (1.0 / (1.0 - ADAM_BETA_TWO**count))
    weights = weights - INNER_RATE * (
        first_hat / (jnp.sqrt(second_hat) + ADAM_EPSILON) + WEIGHT_DECAY * weights
    )
    return (weights, first_moment, second_moment)


def inner_kernel(
    n,
    tokens,
    targets,
    mask,
    gain,
    params,
    moment_one,
    moment_two,
    out,
    xbuf,
    xt,
    tok,
    w,
    m1,
    m2,
    wbf,
    vsend,
    vrecv,
    vown,
    rbuf,
    scale,
    load_sem,
    out_sem,
    x_send,
    x_recv,
    v_send,
    v_recv,
    r_send,
    r_recv,
):
    me = lax.axis_index("fsdp")
    rows, width = tokens.shape
    feat = width // n
    chunks = rows // CHUNK
    blocks = feat // BLOCK
    island_tokens = rows * n

    def peer(k):
        return lax.rem(me + k, n)

    def source(k):
        return lax.rem(me + n - k, n)

    def own_rows(c):
        return pl.ds(pl.multiple_of(me * rows + c * CHUNK, CHUNK), CHUNK)

    def chunk_rows(c):
        return pl.ds(pl.multiple_of(c * CHUNK, CHUNK), CHUNK)

    def x_copy(k, c):
        to = peer(k)
        return pltpu.make_async_remote_copy(
            src_ref=tokens.at[chunk_rows(c), pl.ds(pl.multiple_of(to * feat, 128), feat)],
            dst_ref=xbuf.at[own_rows(c)],
            send_sem=x_send.at[k - 1, c],
            recv_sem=x_recv.at[k - 1, c],
            device_id={"fsdp": to},
            device_id_type=MESH,
        )

    def v_copy(step, k, c):
        return pltpu.make_async_remote_copy(
            src_ref=vsend.at[step, k - 1, chunk_rows(c)],
            dst_ref=vrecv.at[step, k - 1, chunk_rows(c)],
            send_sem=v_send.at[step, k - 1, c],
            recv_sem=v_recv.at[step, k - 1, c],
            device_id={"fsdp": source(k)},
            device_id_type=MESH,
        )

    def r_copy(step, k, c):
        return pltpu.make_async_remote_copy(
            src_ref=rbuf.at[step, own_rows(c)],
            dst_ref=rbuf.at[step, own_rows(c)],
            send_sem=r_send.at[step, k - 1, c],
            recv_sem=r_recv.at[step, k - 1, c],
            device_id={"fsdp": peer(k)},
            device_id_type=MESH,
        )

    def each(body):
        def run(k, carry):
            body(k)
            return carry

        lax.fori_loop(1, n, run, 0)

    barrier = pltpu.get_barrier_semaphore()
    each(
        lambda k: pl.semaphore_signal(
            barrier, inc=1, device_id={"fsdp": peer(k)}, device_id_type=MESH
        )
    )
    pl.semaphore_wait(barrier, n - 1)

    for c in range(chunks):
        each(lambda k: x_copy(k, c).start())

    load_own = pltpu.make_async_copy(
        tokens.at[:, pl.ds(pl.multiple_of(me * feat, 128), feat)],
        xbuf.at[pl.ds(pl.multiple_of(me * rows, CHUNK), rows)],
        load_sem.at[0],
    )
    load_w = pltpu.make_async_copy(params, w, load_sem.at[1])
    load_tok = pltpu.make_async_copy(tokens, tok, load_sem.at[2])
    load_m1 = pltpu.make_async_copy(moment_one, m1, load_sem.at[3])
    load_m2 = pltpu.make_async_copy(moment_two, m2, load_sem.at[4])
    for load in (load_w, load_own, load_tok, load_m1, load_m2):
        load.start()

    load_w.wait()

    def cast_block(b, carry):
        at = pl.ds(pl.multiple_of(b * BLOCK, BLOCK), BLOCK)
        wbf[at, :] = w[at, :].astype(jnp.bfloat16)
        return carry

    lax.fori_loop(0, blocks, cast_block, 0)

    def take_chunk(k, c):
        start = pl.multiple_of(source(k) * rows + c * CHUNK, CHUNK)
        at = pl.ds(start, CHUNK)

        def scale_block(b, carry):
            cols = pl.ds(pl.multiple_of(b * BLOCK, BLOCK), BLOCK)
            gains = gain[:, pl.ds(pl.multiple_of(me * feat + b * BLOCK, BLOCK), BLOCK)]
            scaled = xbuf[at, cols].astype(jnp.float32) * gains
            xbuf[at, cols] = scaled.astype(jnp.bfloat16)
            xt[cols, at] = scaled.T.astype(jnp.bfloat16)
            return carry

        lax.fori_loop(0, blocks, scale_block, 0)
        return jnp.dot(xbuf[at, :], wbf[...], preferred_element_type=jnp.float32)

    def residual(step, c):
        at = chunk_rows(c)
        each(lambda k: v_copy(step, k, c).wait_recv())
        total = vown[step, at, :]
        for k in range(1, n):
            total = total + vrecv[step, k - 1, at, :].astype(jnp.float32)
        row_scale = scale[at, :]
        keep = mask[at, :].astype(jnp.float32)
        goal = targets[at, :].astype(jnp.float32)
        result = row_scale * keep * (row_scale * total - goal) / island_tokens
        rbuf[step, own_rows(c), :] = result.astype(jnp.bfloat16)
        each(lambda k: r_copy(step, k, c).start())

    load_own.wait()
    for c in range(chunks):
        vown[0, chunk_rows(c), :] = take_chunk(0, c)

    load_tok.wait()

    def square(b, total):
        part = tok[:, pl.ds(pl.multiple_of(b * 128, 128), 128)].astype(jnp.float32)
        return total + part * part

    squares = lax.fori_loop(0, width // 128, square, jnp.zeros((rows, 128), jnp.float32))
    mean = jnp.sum(squares, axis=1, keepdims=True) / width
    scale[...] = lax.rsqrt(mean + NORM_EPSILON)
    load_m1.wait()
    load_m2.wait()

    for c in range(chunks):

        def arrive(k):
            x_copy(k, c).wait_recv()
            vsend[0, k - 1, chunk_rows(c), :] = take_chunk(k, c).astype(jnp.bfloat16)
            v_copy(0, k, c).start()

        each(arrive)
        if c:
            residual(0, c - 1)
    residual(0, chunks - 1)

    def update(step):
        for c in range(chunks):
            each(lambda k: r_copy(step, k, c).wait_recv())

        def update_block(b, carry):
            at = pl.ds(pl.multiple_of(b * BLOCK, BLOCK), BLOCK)
            gradient = jnp.dot(xt[at, :], rbuf[step], preferred_element_type=jnp.float32)
            new_w, new_m1, new_m2 = adam_update(
                w[at, :], m1[at, :], m2[at, :], gradient, float(STEP_BASE + step + 1)
            )
            w[at, :] = new_w
            if step == 0:
                m1[at, :] = new_m1
                m2[at, :] = new_m2
                wbf[at, :] = new_w.astype(jnp.bfloat16)
            else:
                pltpu.make_async_copy(w.at[at], out.at[at], out_sem.at[b]).start()
            return carry

        lax.fori_loop(0, blocks, update_block, 0)

    update(0)

    def partial(k, c):
        at = pl.ds(pl.multiple_of(source(k) * rows + c * CHUNK, CHUNK), CHUNK)
        return jnp.dot(xbuf[at, :], wbf[...], preferred_element_type=jnp.float32)

    for c in range(chunks):

        def send(k):
            vsend[1, k - 1, chunk_rows(c), :] = partial(k, c).astype(jnp.bfloat16)
            v_copy(1, k, c).start()

        each(send)
    for c in range(chunks):
        vown[1, chunk_rows(c), :] = partial(0, c)
    for c in range(chunks):
        residual(1, c)
    update(1)

    def finish(b, carry):
        at = pl.ds(pl.multiple_of(b * BLOCK, BLOCK), BLOCK)
        pltpu.make_async_copy(w.at[at], out.at[at], out_sem.at[b]).wait()
        return carry

    lax.fori_loop(0, blocks, finish, 0)
    for c in range(chunks):

        def drain(k):
            x_copy(k, c).wait_send()
            for step in range(2):
                v_copy(step, k, c).wait_send()
                r_copy(step, k, c).wait_send()

        each(drain)


def inner_steps(n, tokens, targets, mask, gain, params, moment_one, moment_two):
    rows, width = tokens.shape
    feat, columns = params.shape
    chunks = rows // CHUNK
    vmem = pl.BlockSpec(memory_space=pltpu.VMEM)
    hbm = pl.BlockSpec(memory_space=pl.ANY)
    dma = pltpu.SemaphoreType.DMA
    bf16, f32 = jnp.bfloat16, jnp.float32
    return pl.pallas_call(
        functools.partial(inner_kernel, n),
        out_shape=jax.ShapeDtypeStruct((feat, columns), f32),
        in_specs=[hbm, vmem, vmem, vmem, hbm, hbm, hbm],
        out_specs=hbm,
        scratch_shapes=[
            pltpu.VMEM((rows * n, feat), bf16),
            pltpu.VMEM((feat, rows * n), bf16),
            pltpu.VMEM((rows, width), bf16),
            pltpu.VMEM((feat, columns), f32),
            pltpu.VMEM((feat, columns), f32),
            pltpu.VMEM((feat, columns), f32),
            pltpu.VMEM((feat, columns), bf16),
            pltpu.VMEM((2, n - 1, rows, columns), bf16),
            pltpu.VMEM((2, n - 1, rows, columns), bf16),
            pltpu.VMEM((2, rows, columns), f32),
            pltpu.VMEM((2, rows * n, columns), bf16),
            pltpu.VMEM((rows, 1), f32),
            dma((5,)),
            dma((feat // BLOCK,)),
            dma((n - 1, chunks)),
            dma((n - 1, chunks)),
            dma((2, n - 1, chunks)),
            dma((2, n - 1, chunks)),
            dma((2, n - 1, chunks)),
            dma((2, n - 1, chunks)),
        ],
        compiler_params=pltpu.CompilerParams(
            collective_id=0, has_side_effects=True, vmem_limit_bytes=56 * 2**20
        ),
        cost_estimate=pl.CostEstimate(
            flops=8 * rows * n * feat * columns,
            bytes_accessed=4 * rows * width + 16 * feat * columns,
            transcendentals=4 * feat * columns,
        ),
    )(tokens, targets, mask, gain, params, moment_one, moment_two)


def per_device(
    tokens,
    targets,
    loss_mask,
    norm_gain,
    params,
    moment_one,
    moment_two,
    outer_delta,
    outer_momentum,
):
    n = lax.axis_size("fsdp")
    island_count = lax.axis_size("island")
    summed = lax.psum(outer_delta[0], "island")
    weights = inner_steps(
        n,
        tokens[0],
        targets[0],
        loss_mask[0][:, None],
        norm_gain[None, :],
        params[0],
        moment_one[0],
        moment_two[0],
    )
    outer_mean = summed / island_count
    momentum_new = OUTER_MOMENTUM * outer_momentum + outer_mean
    outer_update = OUTER_RATE * (outer_mean + OUTER_MOMENTUM * momentum_new)
    return (weights[None], momentum_new, outer_update)


def solution(mesh):
    return jax.shard_map(
        per_device,
        mesh=mesh,
        in_specs=(
            P("island", "fsdp", None),
            P("island", "fsdp", None),
            P("island", "fsdp"),
            P(),
            P("island", "fsdp", None),
            P("island", "fsdp", None),
            P("island", "fsdp", None),
            P("island", "fsdp", None),
            P("fsdp", None),
        ),
        out_specs=(P("island", "fsdp", None), P("fsdp", None), P("fsdp", None)),
        check_vma=False,
    )
```

```python
import functools
import jax
import jax.numpy as jnp
from jax import lax
from jax.experimental import pallas as pl
from jax.experimental.pallas import tpu as pltpu
from jax.sharding import PartitionSpec as P

ADAM_BETA_ONE = 0.9
ADAM_BETA_TWO = 0.95
ADAM_EPSILON = 1e-08
INNER_RATE = 0.005
WEIGHT_DECAY = 0.1
NORM_EPSILON = 1e-05
OUTER_RATE = 0.7
OUTER_MOMENTUM = 0.9
STEP_BASE = 1000
MESH = pl.DeviceIdType.MESH
CHUNK = 128
BLOCK = 256
UNITS = 4
WINDOW = 3


def adam_update(weights, first_moment, second_moment, gradient, count):
    first_moment = ADAM_BETA_ONE * first_moment + (1.0 - ADAM_BETA_ONE) * gradient
    second_moment = ADAM_BETA_TWO * second_moment + (1.0 - ADAM_BETA_TWO) * gradient * gradient
    first_hat = first_moment * (1.0 / (1.0 - ADAM_BETA_ONE**count))
    second_hat = second_moment * (1.0 / (1.0 - ADAM_BETA_TWO**count))
    weights = weights - INNER_RATE * (
        first_hat / (jnp.sqrt(second_hat) + ADAM_EPSILON) + WEIGHT_DECAY * weights
    )
    return (weights, first_moment, second_moment)


def inner_kernel(
    n,
    m,
    tokens,
    targets,
    mask,
    gain,
    params,
    moment_one,
    moment_two,
    delta,
    outer_momentum,
    out,
    momentum_out,
    update_out,
    xbuf,
    xt,
    tok,
    w,
    m1,
    m2,
    wbf,
    vacc,
    vsend,
    vrecv,
    vown,
    rbuf,
    scale,
    keep,
    dbuf,
    total_buf,
    outer_buf,
    load_sem,
    out_sem,
    x_send,
    x_recv,
    v_send,
    v_recv,
    r_send,
    r_recv,
    d_send,
    d_recv,
    a_send,
    a_recv,
):
    me = lax.axis_index("fsdp")
    isle = lax.axis_index("island")
    rows, width = tokens.shape
    feat = width // n
    chunks = rows // CHUNK
    blocks = feat // BLOCK
    unit = feat // UNITS
    island_tokens = rows * n
    slab = delta.shape[0] // m

    def peer(k):
        return lax.rem(me + k, n)

    def source(k):
        return lax.rem(me + n - k, n)

    def own_rows(c):
        return pl.ds(pl.multiple_of(me * rows + c * CHUNK, CHUNK), CHUNK)

    def chunk_rows(c):
        return pl.ds(pl.multiple_of(c * CHUNK, CHUNK), CHUNK)

    def slab_rows(i):
        return pl.ds(pl.multiple_of(i * slab, 8), slab)

    def x_copy(k, u):
        c, q = u // UNITS, u % UNITS
        to = peer(k)
        cols = pl.ds(pl.multiple_of(to * feat + q * unit, 128), unit)
        return pltpu.make_async_remote_copy(
            src_ref=tokens.at[chunk_rows(c), cols],
            dst_ref=xbuf.at[own_rows(c), pl.ds(q * unit, unit)],
            send_sem=x_send.at[k - 1, u],
            recv_sem=x_recv.at[k - 1, u],
            device_id={"fsdp": to},
            device_id_type=MESH,
        )

    def v_copy(step, k, c):
        return pltpu.make_async_remote_copy(
            src_ref=vsend.at[step, k - 1, chunk_rows(c)],
            dst_ref=vrecv.at[step, k - 1, chunk_rows(c)],
            send_sem=v_send.at[step, k - 1, c],
            recv_sem=v_recv.at[step, k - 1, c],
            device_id={"fsdp": source(k)},
            device_id_type=MESH,
        )

    def r_copy(step, k, c):
        return pltpu.make_async_remote_copy(
            src_ref=rbuf.at[step, own_rows(c)],
            dst_ref=rbuf.at[step, own_rows(c)],
            send_sem=r_send.at[step, k - 1, c],
            recv_sem=r_recv.at[step, k - 1, c],
            device_id={"fsdp": peer(k)},
            device_id_type=MESH,
        )

    def d_copy(j):
        to = lax.rem(isle + j, m)
        return pltpu.make_async_remote_copy(
            src_ref=delta.at[slab_rows(to)],
            dst_ref=dbuf.at[j],
            send_sem=d_send.at[j - 1],
            recv_sem=d_recv.at[j - 1],
            device_id={"island": to},
            device_id_type=MESH,
        )

    def a_copy(j):
        return pltpu.make_async_remote_copy(
            src_ref=total_buf.at[slab_rows(isle)],
            dst_ref=total_buf.at[slab_rows(isle)],
            send_sem=a_send.at[j - 1],
            recv_sem=a_recv.at[j - 1],
            device_id={"island": lax.rem(isle + j, m)},
            device_id_type=MESH,
        )

    def each(body, count=n):
        def run(k, carry):
            body(k)
            return carry

        lax.fori_loop(1, count, run, 0)

    barrier = pltpu.get_barrier_semaphore()
    each(
        lambda k: pl.semaphore_signal(
            barrier, inc=1, device_id={"fsdp": peer(k)}, device_id_type=MESH
        )
    )
    each(
        lambda j: pl.semaphore_signal(
            barrier, inc=1, device_id={"island": lax.rem(isle + j, m)}, device_id_type=MESH
        ),
        m,
    )
    pl.semaphore_wait(barrier, n + m - 2)

    last_unit = chunks * UNITS
    for u in range(min(WINDOW, last_unit)):
        each(lambda k: x_copy(k, u).start())

    load_own = pltpu.make_async_copy(
        tokens.at[:, pl.ds(pl.multiple_of(me * feat, 128), feat)],
        xbuf.at[pl.ds(pl.multiple_of(me * rows, CHUNK), rows)],
        load_sem.at[0],
    )
    load_w = pltpu.make_async_copy(params, w, load_sem.at[1])
    load_tok = pltpu.make_async_copy(tokens, tok, load_sem.at[2])
    load_m1 = pltpu.make_async_copy(moment_one, m1, load_sem.at[3])
    load_m2 = pltpu.make_async_copy(moment_two, m2, load_sem.at[4])
    load_d = pltpu.make_async_copy(delta.at[slab_rows(isle)], dbuf.at[0], load_sem.at[5])
    load_outer = pltpu.make_async_copy(outer_momentum, outer_buf, load_sem.at[6])
    load_w.start()
    load_own.start()
    each(lambda j: d_copy(j).start(), m)
    for load in (load_d, load_tok, load_m1, load_m2, load_outer):
        load.start()

    load_w.wait()

    def cast_block(b, carry):
        at = pl.ds(pl.multiple_of(b * BLOCK, BLOCK), BLOCK)
        wbf[at, :] = w[at, :].astype(jnp.bfloat16)
        return carry

    lax.fori_loop(0, blocks, cast_block, 0)

    def take_unit(k, u):
        c, q = u // UNITS, u % UNITS
        at = pl.ds(pl.multiple_of(source(k) * rows + c * CHUNK, CHUNK), CHUNK)
        for b in range(unit // 128):
            first = q * unit + b * 128
            cols = pl.ds(first, 128)
            gains = gain[:, pl.ds(pl.multiple_of(me * feat + first, 128), 128)]
            scaled = xbuf[at, cols].astype(jnp.float32) * gains
            xbuf[at, cols] = scaled.astype(jnp.bfloat16)
            xt[cols, at] = scaled.T.astype(jnp.bfloat16)
        cols = pl.ds(q * unit, unit)
        part = jnp.dot(xbuf[at, cols], wbf[cols, :], preferred_element_type=jnp.float32)
        return part if q == 0 else vacc[k] + part

    def residual(step, c):
        at = chunk_rows(c)
        each(lambda k: v_copy(step, k, c).wait_recv())
        total = vown[step, at, :]
        for k in range(1, n):
            total = total + vrecv[step, k - 1, at, :].astype(jnp.float32)
        row_scale = scale[at, :]
        goal = targets[at, :].astype(jnp.float32)
        result = row_scale * keep[at, :] * (row_scale * total - goal) / island_tokens
        rbuf[step, own_rows(c), :] = result.astype(jnp.bfloat16)
        each(lambda k: r_copy(step, k, c).start())

    load_own.wait()
    for u in range(last_unit):
        if u % UNITS == UNITS - 1:
            vown[0, chunk_rows(u // UNITS), :] = take_unit(0, u)
        else:
            vacc[0] = take_unit(0, u)

    load_d.wait()
    each(lambda j: d_copy(j).wait_recv(), m)
    total_buf[slab_rows(isle), :] = lax.fori_loop(
        1, m, lambda j, total: total + dbuf[j], dbuf[0]
    )
    each(lambda j: a_copy(j).start(), m)

    load_tok.wait()

    def square(b, total):
        part = tok[:, pl.ds(pl.multiple_of(b * 128, 128), 128)].astype(jnp.float32)
        return total + part * part

    squares = lax.fori_loop(0, width // 128, square, jnp.zeros((rows, 128), jnp.float32))
    mean = jnp.sum(squares, axis=1, keepdims=True) / width
    scale[...] = lax.rsqrt(mean + NORM_EPSILON)
    keep_row = jnp.broadcast_to(mask[...].astype(jnp.float32), (128, rows))
    keep[...] = keep_row.T[:, :1]
    load_m1.wait()
    load_m2.wait()
    load_outer.wait()

    def outer_copies():
        return (
            pltpu.make_async_copy(outer_buf, momentum_out, load_sem.at[7]),
            pltpu.make_async_copy(total_buf, update_out, load_sem.at[8]),
        )

    def outer_step():
        each(lambda j: a_copy(j).wait_recv(), m)
        each(lambda j: a_copy(j).wait_send(), m)

        def outer_block(b, carry):
            at = pl.ds(pl.multiple_of(b * BLOCK, BLOCK), BLOCK)
            outer_mean = total_buf[at, :] / m
            momentum_new = OUTER_MOMENTUM * outer_buf[at, :] + outer_mean
            outer_buf[at, :] = momentum_new
            total_buf[at, :] = OUTER_RATE * (outer_mean + OUTER_MOMENTUM * momentum_new)
            return carry

        lax.fori_loop(0, blocks, outer_block, 0)
        for copy in outer_copies():
            copy.start()

    for u in range(last_unit):
        c, q = u // UNITS, u % UNITS

        def arrive(k):
            x_copy(k, u).wait_recv()
            if u + WINDOW < last_unit:
                x_copy(k, u + WINDOW).start()
            part = take_unit(k, u)
            if q == UNITS - 1:
                vsend[0, k - 1, chunk_rows(c), :] = part.astype(jnp.bfloat16)
                v_copy(0, k, c).start()
            else:
                vacc[k] = part

        each(arrive)
        if u == UNITS - 1:
            outer_step()
        if c and q == UNITS // 2:
            residual(0, c - 1)
    residual(0, chunks - 1)

    def update(step):
        for c in range(chunks):
            each(lambda k: r_copy(step, k, c).wait_recv())

        def update_block(b, carry):
            at = pl.ds(pl.multiple_of(b * BLOCK, BLOCK), BLOCK)
            gradient = jnp.dot(xt[at, :], rbuf[step], preferred_element_type=jnp.float32)
            new_w, new_m1, new_m2 = adam_update(
                w[at, :], m1[at, :], m2[at, :], gradient, float(STEP_BASE + step + 1)
            )
            w[at, :] = new_w
            if step == 0:
                m1[at, :] = new_m1
                m2[at, :] = new_m2
                wbf[at, :] = new_w.astype(jnp.bfloat16)
            else:
                pltpu.make_async_copy(w.at[at], out.at[at], out_sem.at[b]).start()
            return carry

        lax.fori_loop(0, blocks, update_block, 0)

    update(0)

    def partial(k):
        at = pl.ds(pl.multiple_of(source(k) * rows, CHUNK), rows)
        return jnp.dot(xbuf[at, :], wbf[...], preferred_element_type=jnp.float32)

    def send(k):
        vsend[1, k - 1] = partial(k).astype(jnp.bfloat16)
        for c in range(chunks):
            v_copy(1, k, c).start()

    each(send)
    vown[1] = partial(0)
    for c in range(chunks):
        residual(1, c)
    update(1)

    def finish(b, carry):
        at = pl.ds(pl.multiple_of(b * BLOCK, BLOCK), BLOCK)
        pltpu.make_async_copy(w.at[at], out.at[at], out_sem.at[b]).wait()
        return carry

    lax.fori_loop(0, blocks, finish, 0)
    for copy in outer_copies():
        copy.wait()

    def drain(k):
        for u in range(last_unit):
            x_copy(k, u).wait_send()
        for c in range(chunks):
            for step in range(2):
                v_copy(step, k, c).wait_send()
                r_copy(step, k, c).wait_send()

    each(drain)
    each(lambda j: d_copy(j).wait_send(), m)


def train(n, m, tokens, targets, mask, gain, params, moment_one, moment_two, delta, momentum):
    rows, width = tokens.shape
    feat, columns = params.shape
    chunks = rows // CHUNK
    slab = delta.shape[0] // m
    vmem = pl.BlockSpec(memory_space=pltpu.VMEM)
    hbm = pl.BlockSpec(memory_space=pl.ANY)
    dma = pltpu.SemaphoreType.DMA
    bf16, f32 = jnp.bfloat16, jnp.float32
    return pl.pallas_call(
        functools.partial(inner_kernel, n, m),
        out_shape=(
            jax.ShapeDtypeStruct((feat, columns), f32),
            jax.ShapeDtypeStruct(momentum.shape, f32),
            jax.ShapeDtypeStruct(momentum.shape, f32),
        ),
        in_specs=[hbm, vmem, vmem, vmem, hbm, hbm, hbm, hbm, hbm],
        out_specs=(hbm, hbm, hbm),
        scratch_shapes=[
            pltpu.VMEM((rows * n, feat), bf16),
            pltpu.VMEM((feat, rows * n), bf16),
            pltpu.VMEM((rows, width), bf16),
            pltpu.VMEM((feat, columns), f32),
            pltpu.VMEM((feat, columns), f32),
            pltpu.VMEM((feat, columns), f32),
            pltpu.VMEM((feat, columns), bf16),
            pltpu.VMEM((n, CHUNK, columns), f32),
            pltpu.VMEM((2, n - 1, rows, columns), bf16),
            pltpu.VMEM((2, n - 1, rows, columns), bf16),
            pltpu.VMEM((2, rows, columns), f32),
            pltpu.VMEM((2, rows * n, columns), bf16),
            pltpu.VMEM((rows, 1), f32),
            pltpu.VMEM((rows, 1), f32),
            pltpu.VMEM((m, slab, delta.shape[1]), f32),
            pltpu.VMEM(delta.shape, f32),
            pltpu.VMEM(delta.shape, f32),
            dma((9,)),
            dma((feat // BLOCK,)),
            dma((n - 1, chunks * UNITS)),
            dma((n - 1, chunks * UNITS)),
            dma((2, n - 1, chunks)),
            dma((2, n - 1, chunks)),
            dma((2, n - 1, chunks)),
            dma((2, n - 1, chunks)),
            dma((m - 1,)),
            dma((m - 1,)),
            dma((m - 1,)),
            dma((m - 1,)),
        ],
        compiler_params=pltpu.CompilerParams(
            collective_id=0, has_side_effects=True, vmem_limit_bytes=56 * 2**20
        ),
        cost_estimate=pl.CostEstimate(
            flops=8 * rows * n * feat * columns,
            bytes_accessed=4 * rows * width + 16 * feat * columns,
            transcendentals=4 * feat * columns,
        ),
    )(tokens, targets, mask, gain, params, moment_one, moment_two, delta, momentum)


def per_device(
    tokens,
    targets,
    loss_mask,
    norm_gain,
    params,
    moment_one,
    moment_two,
    outer_delta,
    outer_momentum,
):
    weights, momentum_new, outer_update = train(
        lax.axis_size("fsdp"),
        lax.axis_size("island"),
        tokens[0],
        targets[0],
        loss_mask,
        norm_gain[None, :],
        params[0],
        moment_one[0],
        moment_two[0],
        outer_delta[0],
        outer_momentum,
    )
    return (weights[None], momentum_new, outer_update)


def solution(mesh):
    return jax.shard_map(
        per_device,
        mesh=mesh,
        in_specs=(
            P("island", "fsdp", None),
            P("island", "fsdp", None),
            P("island", "fsdp"),
            P(),
            P("island", "fsdp", None),
            P("island", "fsdp", None),
            P("island", "fsdp", None),
            P("island", "fsdp", None),
            P("fsdp", None),
        ),
        out_specs=(P("island", "fsdp", None), P("fsdp", None), P("fsdp", None)),
        check_vma=False,
    )
```

```python
import functools
import jax
import jax.numpy as jnp
from jax import lax
from jax.experimental import pallas as pl
from jax.experimental.pallas import tpu as pltpu
from jax.sharding import PartitionSpec as P

ADAM_BETA_ONE = 0.9
ADAM_BETA_TWO = 0.95
ADAM_EPSILON = 1e-08
INNER_RATE = 0.005
WEIGHT_DECAY = 0.1
NORM_EPSILON = 1e-05
OUTER_RATE = 0.7
OUTER_MOMENTUM = 0.9
STEP_BASE = 1000
MESH = pl.DeviceIdType.MESH
CHUNK = 64
BLOCK = 256
UNITS = 2
WINDOW = 3


def adam_update(weights, first_moment, second_moment, gradient, count):
    first_moment = ADAM_BETA_ONE * first_moment + (1.0 - ADAM_BETA_ONE) * gradient
    second_moment = ADAM_BETA_TWO * second_moment + (1.0 - ADAM_BETA_TWO) * gradient * gradient
    first_hat = first_moment * (1.0 / (1.0 - ADAM_BETA_ONE**count))
    second_hat = second_moment * (1.0 / (1.0 - ADAM_BETA_TWO**count))
    weights = weights - INNER_RATE * (
        first_hat / (jnp.sqrt(second_hat) + ADAM_EPSILON) + WEIGHT_DECAY * weights
    )
    return (weights, first_moment, second_moment)


def inner_kernel(
    n,
    m,
    tokens,
    targets,
    mask,
    gain,
    params,
    moment_one,
    moment_two,
    delta,
    outer_momentum,
    out,
    momentum_out,
    update_out,
    xbuf,
    xt,
    tok,
    w,
    m1,
    m2,
    wbf,
    vacc,
    vsend,
    vrecv,
    vown,
    rbuf,
    scale,
    keep,
    dbuf,
    total_buf,
    outer_buf,
    load_sem,
    x_send,
    x_recv,
    v_send,
    v_recv,
    r_send,
    r_recv,
    d_send,
    d_recv,
    a_send,
    a_recv,
):
    me = lax.axis_index("fsdp")
    isle = lax.axis_index("island")
    rows, width = tokens.shape
    feat = width // n
    chunks = rows // CHUNK
    blocks = feat // BLOCK
    unit = feat // UNITS
    island_tokens = rows * n
    slab = delta.shape[0] // m

    def peer(k):
        return lax.rem(me + k, n)

    def source(k):
        return lax.rem(me + n - k, n)

    def own_rows(c):
        return pl.ds(pl.multiple_of(me * rows + c * CHUNK, CHUNK), CHUNK)

    def chunk_rows(c):
        return pl.ds(pl.multiple_of(c * CHUNK, CHUNK), CHUNK)

    def slab_rows(i):
        return pl.ds(pl.multiple_of(i * slab, 8), slab)

    def x_copy(k, u):
        c, q = u // UNITS, u % UNITS
        to = peer(k)
        cols = pl.ds(pl.multiple_of(to * feat + q * unit, 128), unit)
        return pltpu.make_async_remote_copy(
            src_ref=tokens.at[chunk_rows(c), cols],
            dst_ref=xbuf.at[own_rows(c), pl.ds(q * unit, unit)],
            send_sem=x_send.at[k - 1, u],
            recv_sem=x_recv.at[k - 1, u],
            device_id={"fsdp": to},
            device_id_type=MESH,
        )

    def v_copy(step, k, c):
        return pltpu.make_async_remote_copy(
            src_ref=vsend.at[step, k - 1, chunk_rows(c)],
            dst_ref=vrecv.at[step, k - 1, chunk_rows(c)],
            send_sem=v_send.at[step, k - 1, c],
            recv_sem=v_recv.at[step, k - 1, c],
            device_id={"fsdp": source(k)},
            device_id_type=MESH,
        )

    def r_copy(step, k, c):
        return pltpu.make_async_remote_copy(
            src_ref=rbuf.at[step, own_rows(c)],
            dst_ref=rbuf.at[step, own_rows(c)],
            send_sem=r_send.at[step, k - 1, c],
            recv_sem=r_recv.at[step, k - 1, c],
            device_id={"fsdp": peer(k)},
            device_id_type=MESH,
        )

    def d_copy(j):
        to = lax.rem(isle + j, m)
        return pltpu.make_async_remote_copy(
            src_ref=delta.at[slab_rows(to)],
            dst_ref=dbuf.at[j],
            send_sem=d_send.at[j - 1],
            recv_sem=d_recv.at[j - 1],
            device_id={"island": to},
            device_id_type=MESH,
        )

    def a_copy(j):
        return pltpu.make_async_remote_copy(
            src_ref=total_buf.at[slab_rows(isle)],
            dst_ref=total_buf.at[slab_rows(isle)],
            send_sem=a_send.at[j - 1],
            recv_sem=a_recv.at[j - 1],
            device_id={"island": lax.rem(isle + j, m)},
            device_id_type=MESH,
        )

    def each(body, count=n):
        def run(k, carry):
            body(k)
            return carry

        lax.fori_loop(1, count, run, 0)

    barrier = pltpu.get_barrier_semaphore()
    each(
        lambda k: pl.semaphore_signal(
            barrier, inc=1, device_id={"fsdp": peer(k)}, device_id_type=MESH
        )
    )
    each(
        lambda j: pl.semaphore_signal(
            barrier, inc=1, device_id={"island": lax.rem(isle + j, m)}, device_id_type=MESH
        ),
        m,
    )
    pl.semaphore_wait(barrier, n + m - 2)

    last_unit = chunks * UNITS
    for u in range(min(WINDOW, last_unit)):
        each(lambda k: x_copy(k, u).start())

    load_own = pltpu.make_async_copy(
        tokens.at[:, pl.ds(pl.multiple_of(me * feat, 128), feat)],
        xbuf.at[pl.ds(pl.multiple_of(me * rows, CHUNK), rows)],
        load_sem.at[0],
    )
    load_w = pltpu.make_async_copy(params, w, load_sem.at[1])
    load_tok = pltpu.make_async_copy(tokens, tok, load_sem.at[2])
    load_m1 = pltpu.make_async_copy(moment_one, m1, load_sem.at[3])
    load_m2 = pltpu.make_async_copy(moment_two, m2, load_sem.at[4])
    load_d = pltpu.make_async_copy(delta.at[slab_rows(isle)], dbuf.at[0], load_sem.at[5])
    load_outer = pltpu.make_async_copy(outer_momentum, outer_buf, load_sem.at[6])
    load_w.start()
    load_own.start()
    each(lambda j: d_copy(j).start(), m)
    for load in (load_d, load_tok, load_m1, load_m2, load_outer):
        load.start()

    load_w.wait()

    def cast_block(b, carry):
        at = pl.ds(pl.multiple_of(b * BLOCK, BLOCK), BLOCK)
        wbf[at, :] = w[at, :].astype(jnp.bfloat16)
        return carry

    lax.fori_loop(0, blocks, cast_block, 0)

    def take_unit(k, u):
        c, q = u // UNITS, u % UNITS
        at = pl.ds(pl.multiple_of(source(k) * rows + c * CHUNK, CHUNK), CHUNK)
        for b in range(unit // 128):
            first = q * unit + b * 128
            cols = pl.ds(first, 128)
            gains = gain[:, pl.ds(pl.multiple_of(me * feat + first, 128), 128)]
            scaled = xbuf[at, cols].astype(jnp.float32) * gains
            xbuf[at, cols] = scaled.astype(jnp.bfloat16)
        cols = pl.ds(q * unit, unit)
        part = jnp.dot(xbuf[at, cols], wbf[cols, :], preferred_element_type=jnp.float32)
        return part if q == 0 else vacc[k] + part

    def turn_unit(k, u):
        c, q = u // UNITS, u % UNITS
        if c % 2:
            start = source(k) * rows + (c - 1) * CHUNK
            at = pl.ds(pl.multiple_of(start, 2 * CHUNK), 2 * CHUNK)
            for b in range(unit // 128):
                cols = pl.ds(q * unit + b * 128, 128)
                xt[cols, at] = xbuf[at, cols].astype(jnp.float32).T.astype(jnp.bfloat16)

    def residual(step, c):
        at = chunk_rows(c)
        each(lambda k: v_copy(step, k, c).wait_recv())
        total = vown[step, at, :]
        for k in range(1, n):
            total = total + vrecv[step, k - 1, at, :].astype(jnp.float32)
        row_scale = scale[at, :]
        goal = targets[at, :].astype(jnp.float32)
        result = row_scale * keep[at, :] * (row_scale * total - goal) / island_tokens
        rbuf[step, own_rows(c), :] = result.astype(jnp.bfloat16)
        each(lambda k: r_copy(step, k, c).start())

    load_own.wait()
    for u in range(last_unit):
        if u % UNITS == UNITS - 1:
            vown[0, chunk_rows(u // UNITS), :] = take_unit(0, u)
        else:
            vacc[0] = take_unit(0, u)
        turn_unit(0, u)

    load_d.wait()
    each(lambda j: d_copy(j).wait_recv(), m)
    total_buf[slab_rows(isle), :] = lax.fori_loop(
        1, m, lambda j, total: total + dbuf[j], dbuf[0]
    )
    each(lambda j: a_copy(j).start(), m)

    load_tok.wait()

    def square(b, total):
        part = tok[:, pl.ds(pl.multiple_of(b * 128, 128), 128)].astype(jnp.float32)
        return total + part * part

    squares = lax.fori_loop(0, width // 128, square, jnp.zeros((rows, 128), jnp.float32))
    mean = jnp.sum(squares, axis=1, keepdims=True) / width
    scale[...] = lax.rsqrt(mean + NORM_EPSILON)
    keep_row = jnp.broadcast_to(mask[...].astype(jnp.float32), (128, rows))
    keep[...] = keep_row.T[:, :1]
    load_m1.wait()
    load_m2.wait()
    load_outer.wait()

    def outer_step():
        each(lambda j: a_copy(j).wait_recv(), m)
        each(lambda j: a_copy(j).wait_send(), m)

        def outer_block(b, carry):
            at = pl.ds(pl.multiple_of(b * BLOCK, BLOCK), BLOCK)
            outer_mean = total_buf[at, :] / m
            momentum_new = OUTER_MOMENTUM * outer_buf[at, :] + outer_mean
            momentum_out[at, :] = momentum_new
            update_out[at, :] = OUTER_RATE * (outer_mean + OUTER_MOMENTUM * momentum_new)
            return carry

        lax.fori_loop(0, blocks, outer_block, 0)

    for u in range(last_unit):
        c, q = u // UNITS, u % UNITS

        def arrive(k):
            x_copy(k, u).wait_recv()
            if u + WINDOW < last_unit:
                x_copy(k, u + WINDOW).start()
            part = take_unit(k, u)
            if q == UNITS - 1:
                vsend[0, k - 1, chunk_rows(c), :] = part.astype(jnp.bfloat16)
                v_copy(0, k, c).start()
            else:
                vacc[k] = part
            turn_unit(k, u)

        each(arrive)
        if u == UNITS - 1:
            outer_step()
        if c and q == (0 if c == chunks - 1 else UNITS - 1):
            residual(0, c - 1)
    residual(0, chunks - 1)

    def update(step):
        for c in range(chunks):
            each(lambda k: r_copy(step, k, c).wait_recv())

        def update_block(b, carry):
            at = pl.ds(pl.multiple_of(b * BLOCK, BLOCK), BLOCK)
            gradient = jnp.dot(xt[at, :], rbuf[step], preferred_element_type=jnp.float32)
            new_w, new_m1, new_m2 = adam_update(
                w[at, :], m1[at, :], m2[at, :], gradient, float(STEP_BASE + step + 1)
            )
            if step == 0:
                w[at, :] = new_w
                m1[at, :] = new_m1
                m2[at, :] = new_m2
                wbf[at, :] = new_w.astype(jnp.bfloat16)
            else:
                out[at, :] = new_w
            return carry

        lax.fori_loop(0, blocks, update_block, 0)

    update(0)

    def partial(k):
        at = pl.ds(pl.multiple_of(source(k) * rows, CHUNK), rows)
        return jnp.dot(xbuf[at, :], wbf[...], preferred_element_type=jnp.float32)

    def send(k):
        vsend[1, k - 1] = partial(k).astype(jnp.bfloat16)
        for c in range(chunks):
            v_copy(1, k, c).start()

    each(send)
    vown[1] = partial(0)
    for c in range(chunks):
        residual(1, c)
    update(1)

    def drain(k):
        for u in range(last_unit):
            x_copy(k, u).wait_send()
        for c in range(chunks):
            for step in range(2):
                v_copy(step, k, c).wait_send()
                r_copy(step, k, c).wait_send()

    each(drain)
    each(lambda j: d_copy(j).wait_send(), m)


def train(n, m, tokens, targets, mask, gain, params, moment_one, moment_two, delta, momentum):
    rows, width = tokens.shape
    feat, columns = params.shape
    chunks = rows // CHUNK
    slab = delta.shape[0] // m
    vmem = pl.BlockSpec(memory_space=pltpu.VMEM)
    hbm = pl.BlockSpec(memory_space=pl.ANY)
    dma = pltpu.SemaphoreType.DMA
    bf16, f32 = jnp.bfloat16, jnp.float32
    return pl.pallas_call(
        functools.partial(inner_kernel, n, m),
        out_shape=(
            pltpu.VMEM((feat, columns), f32),
            pltpu.VMEM(momentum.shape, f32),
            pltpu.VMEM(momentum.shape, f32),
        ),
        in_specs=[hbm, vmem, vmem, vmem, hbm, hbm, hbm, hbm, hbm],
        out_specs=(vmem, vmem, vmem),
        scratch_shapes=[
            pltpu.VMEM((rows * n, feat), bf16),
            pltpu.VMEM((feat, rows * n), bf16),
            pltpu.VMEM((rows, width), bf16),
            pltpu.VMEM((feat, columns), f32),
            pltpu.VMEM((feat, columns), f32),
            pltpu.VMEM((feat, columns), f32),
            pltpu.VMEM((feat, columns), bf16),
            pltpu.VMEM((n, CHUNK, columns), f32),
            pltpu.VMEM((2, n - 1, rows, columns), bf16),
            pltpu.VMEM((2, n - 1, rows, columns), bf16),
            pltpu.VMEM((2, rows, columns), f32),
            pltpu.VMEM((2, rows * n, columns), bf16),
            pltpu.VMEM((rows, 1), f32),
            pltpu.VMEM((rows, 1), f32),
            pltpu.VMEM((m, slab, delta.shape[1]), f32),
            pltpu.VMEM(delta.shape, f32),
            pltpu.VMEM(delta.shape, f32),
            dma((7,)),
            dma((n - 1, chunks * UNITS)),
            dma((n - 1, chunks * UNITS)),
            dma((2, n - 1, chunks)),
            dma((2, n - 1, chunks)),
            dma((2, n - 1, chunks)),
            dma((2, n - 1, chunks)),
            dma((m - 1,)),
            dma((m - 1,)),
            dma((m - 1,)),
            dma((m - 1,)),
        ],
        compiler_params=pltpu.CompilerParams(
            collective_id=0, has_side_effects=True, vmem_limit_bytes=54 * 2**20
        ),
        cost_estimate=pl.CostEstimate(
            flops=8 * rows * n * feat * columns,
            bytes_accessed=4 * rows * width + 16 * feat * columns,
            transcendentals=4 * feat * columns,
        ),
    )(tokens, targets, mask, gain, params, moment_one, moment_two, delta, momentum)


def per_device(
    tokens,
    targets,
    loss_mask,
    norm_gain,
    params,
    moment_one,
    moment_two,
    outer_delta,
    outer_momentum,
):
    weights, momentum_new, outer_update = train(
        lax.axis_size("fsdp"),
        lax.axis_size("island"),
        tokens[0],
        targets[0],
        loss_mask,
        norm_gain[None, :],
        params[0],
        moment_one[0],
        moment_two[0],
        outer_delta[0],
        outer_momentum,
    )
    return (weights[None], momentum_new, outer_update)


def solution(mesh):
    return jax.shard_map(
        per_device,
        mesh=mesh,
        in_specs=(
            P("island", "fsdp", None),
            P("island", "fsdp", None),
            P("island", "fsdp"),
            P(),
            P("island", "fsdp", None),
            P("island", "fsdp", None),
            P("island", "fsdp", None),
            P("island", "fsdp", None),
            P("fsdp", None),
        ),
        out_specs=(P("island", "fsdp", None), P("fsdp", None), P("fsdp", None)),
        check_vma=False,
    )
```

```python
import functools
import jax
import jax.numpy as jnp
from jax import lax
from jax.experimental import pallas as pl
from jax.experimental.pallas import tpu as pltpu
from jax.sharding import PartitionSpec as P

ADAM_BETA_ONE = 0.9
ADAM_BETA_TWO = 0.95
ADAM_EPSILON = 1e-08
INNER_RATE = 0.005
WEIGHT_DECAY = 0.1
NORM_EPSILON = 1e-05
OUTER_RATE = 0.7
OUTER_MOMENTUM = 0.9
STEP_BASE = 1000
MESH = pl.DeviceIdType.MESH
CHUNK = 64
BLOCK = 256
UNITS = 2
WINDOW = 3


def adam_update(weights, first_moment, second_moment, gradient, count):
    first_moment = ADAM_BETA_ONE * first_moment + (1.0 - ADAM_BETA_ONE) * gradient
    second_moment = ADAM_BETA_TWO * second_moment + (1.0 - ADAM_BETA_TWO) * gradient * gradient
    first_hat = first_moment * (1.0 / (1.0 - ADAM_BETA_ONE**count))
    second_hat = second_moment * (1.0 / (1.0 - ADAM_BETA_TWO**count))
    weights = weights - INNER_RATE * (
        first_hat / (second_hat * lax.rsqrt(second_hat) + ADAM_EPSILON) + WEIGHT_DECAY * weights
    )
    return (weights, first_moment, second_moment)


def inner_kernel(
    n,
    m,
    tokens,
    targets,
    mask,
    gain,
    params,
    moment_one,
    moment_two,
    delta,
    outer_momentum,
    out,
    momentum_out,
    update_out,
    xbuf,
    xt,
    tok,
    w,
    m1,
    m2,
    wbf,
    vacc,
    vsend,
    vrecv,
    vown,
    vcross,
    gbuf,
    rbuf,
    scale,
    keep,
    dbuf,
    total_buf,
    outer_buf,
    load_sem,
    x_send,
    x_recv,
    v_send,
    v_recv,
    r_send,
    r_recv,
    d_send,
    d_recv,
    a_send,
    a_recv,
):
    me = lax.axis_index("fsdp")
    isle = lax.axis_index("island")
    rows, width = tokens.shape
    feat = width // n
    chunks = rows // CHUNK
    blocks = feat // BLOCK
    unit = feat // UNITS
    island_tokens = rows * n
    slab = delta.shape[0] // m

    def peer(k):
        return lax.rem(me + k, n)

    def source(k):
        return lax.rem(me + n - k, n)

    def own_rows(c):
        return pl.ds(pl.multiple_of(me * rows + c * CHUNK, CHUNK), CHUNK)

    def chunk_rows(c):
        return pl.ds(pl.multiple_of(c * CHUNK, CHUNK), CHUNK)

    def slab_rows(i):
        return pl.ds(pl.multiple_of(i * slab, 8), slab)

    def x_copy(k, u):
        c, q = u // UNITS, u % UNITS
        to = peer(k)
        cols = pl.ds(pl.multiple_of(to * feat + q * unit, 128), unit)
        return pltpu.make_async_remote_copy(
            src_ref=tokens.at[chunk_rows(c), cols],
            dst_ref=xbuf.at[own_rows(c), pl.ds(q * unit, unit)],
            send_sem=x_send.at[k - 1, u],
            recv_sem=x_recv.at[k - 1, u],
            device_id={"fsdp": to},
            device_id_type=MESH,
        )

    def v_copy(step, k, c):
        return pltpu.make_async_remote_copy(
            src_ref=vsend.at[step, k - 1, chunk_rows(c)],
            dst_ref=vrecv.at[step, k - 1, chunk_rows(c)],
            send_sem=v_send.at[step, k - 1, c],
            recv_sem=v_recv.at[step, k - 1, c],
            device_id={"fsdp": source(k)},
            device_id_type=MESH,
        )

    def r_copy(step, k, c):
        return pltpu.make_async_remote_copy(
            src_ref=rbuf.at[step, own_rows(c)],
            dst_ref=rbuf.at[step, own_rows(c)],
            send_sem=r_send.at[step, k - 1, c],
            recv_sem=r_recv.at[step, k - 1, c],
            device_id={"fsdp": peer(k)},
            device_id_type=MESH,
        )

    paired = n == 4
    partner = me + 1 - 2 * lax.rem(me, 2)
    across = lax.rem(me + 2, 4)
    k_partner = 3 - 2 * lax.rem(me, 2)
    k_far = 4 - k_partner

    def pair_v(step, j, c):
        return pltpu.make_async_remote_copy(
            src_ref=vsend.at[step, j, chunk_rows(c)],
            dst_ref=vrecv.at[step, j, chunk_rows(c)],
            send_sem=v_send.at[step, j, c],
            recv_sem=v_recv.at[step, j, c],
            device_id={"fsdp": across if j == 2 else partner},
            device_id_type=MESH,
        )

    def pair_r(step, j, c):
        owner = across if j == 2 else me
        at = pl.ds(pl.multiple_of(owner * rows + c * CHUNK, CHUNK), CHUNK)
        return pltpu.make_async_remote_copy(
            src_ref=rbuf.at[step, at],
            dst_ref=rbuf.at[step, at],
            send_sem=r_send.at[step, j, c],
            recv_sem=r_recv.at[step, j, c],
            device_id={"fsdp": across if j == 1 else partner},
            device_id_type=MESH,
        )

    def d_copy(j):
        to = lax.rem(isle + j, m)
        return pltpu.make_async_remote_copy(
            src_ref=delta.at[slab_rows(to)],
            dst_ref=dbuf.at[j],
            send_sem=d_send.at[j - 1],
            recv_sem=d_recv.at[j - 1],
            device_id={"island": to},
            device_id_type=MESH,
        )

    def a_copy(j):
        return pltpu.make_async_remote_copy(
            src_ref=total_buf.at[slab_rows(isle)],
            dst_ref=total_buf.at[slab_rows(isle)],
            send_sem=a_send.at[j - 1],
            recv_sem=a_recv.at[j - 1],
            device_id={"island": lax.rem(isle + j, m)},
            device_id_type=MESH,
        )

    def each(body, count=n):
        def run(k, carry):
            body(k)
            return carry

        lax.fori_loop(1, count, run, 0)

    barrier = pltpu.get_barrier_semaphore()
    each(
        lambda k: pl.semaphore_signal(
            barrier, inc=1, device_id={"fsdp": peer(k)}, device_id_type=MESH
        )
    )
    each(
        lambda j: pl.semaphore_signal(
            barrier, inc=1, device_id={"island": lax.rem(isle + j, m)}, device_id_type=MESH
        ),
        m,
    )
    pl.semaphore_wait(barrier, n + m - 2)

    last_unit = chunks * UNITS
    for u in range(min(WINDOW, last_unit)):
        each(lambda k: x_copy(k, u).start())

    load_own = pltpu.make_async_copy(
        tokens.at[:, pl.ds(pl.multiple_of(me * feat, 128), feat)],
        xbuf.at[pl.ds(pl.multiple_of(me * rows, CHUNK), rows)],
        load_sem.at[0],
    )
    load_w = pltpu.make_async_copy(params, w, load_sem.at[1])
    load_tok = pltpu.make_async_copy(tokens, tok, load_sem.at[2])
    load_m1 = pltpu.make_async_copy(moment_one, m1, load_sem.at[3])
    load_m2 = pltpu.make_async_copy(moment_two, m2, load_sem.at[4])
    load_d = pltpu.make_async_copy(delta.at[slab_rows(isle)], dbuf.at[0], load_sem.at[5])
    load_outer = pltpu.make_async_copy(outer_momentum, outer_buf, load_sem.at[6])
    load_w.start()
    load_own.start()
    each(lambda j: d_copy(j).start(), m)
    for load in (load_d, load_tok, load_m1, load_m2, load_outer):
        load.start()

    load_w.wait()

    def cast_block(b, carry):
        at = pl.ds(pl.multiple_of(b * BLOCK, BLOCK), BLOCK)
        wbf[at, :] = w[at, :].astype(jnp.bfloat16)
        return carry

    lax.fori_loop(0, blocks, cast_block, 0)

    def take_unit(k, u):
        c, q = u // UNITS, u % UNITS
        at = pl.ds(pl.multiple_of(source(k) * rows + c * CHUNK, CHUNK), CHUNK)
        for b in range(unit // 128):
            first = q * unit + b * 128
            cols = pl.ds(first, 128)
            gains = gain[:, pl.ds(pl.multiple_of(me * feat + first, 128), 128)]
            scaled = xbuf[at, cols].astype(jnp.float32) * gains
            xbuf[at, cols] = scaled.astype(jnp.bfloat16)
        cols = pl.ds(q * unit, unit)
        part = jnp.dot(xbuf[at, cols], wbf[cols, :], preferred_element_type=jnp.float32)
        return part if q == 0 else vacc[k] + part

    def turn_unit(k, u):
        c, q = u // UNITS, u % UNITS
        if c % 2:
            start = source(k) * rows + (c - 1) * CHUNK
            at = pl.ds(pl.multiple_of(start, 2 * CHUNK), 2 * CHUNK)
            for b in range(unit // 128):
                cols = pl.ds(q * unit + b * 128, 128)
                xt[cols, at] = xbuf[at, cols].astype(jnp.float32).T.astype(jnp.bfloat16)

    def combine(step, c):
        if paired:
            at = chunk_rows(c)
            pair_v(step, 1, c).wait_recv()
            both = vcross[step, at, :] + vrecv[step, 1, at, :].astype(jnp.float32)
            vsend[step, 2, at, :] = both.astype(jnp.bfloat16)
            pair_v(step, 2, c).start()

    def residual(step, c):
        at = chunk_rows(c)
        total = vown[step, at, :]
        if paired:
            for j in (0, 2):
                pair_v(step, j, c).wait_recv()
                total = total + vrecv[step, j, at, :].astype(jnp.float32)
        else:
            each(lambda k: v_copy(step, k, c).wait_recv())
            for k in range(1, n):
                total = total + vrecv[step, k - 1, at, :].astype(jnp.float32)
        row_scale = scale[at, :]
        goal = targets[at, :].astype(jnp.float32)
        result = row_scale * keep[at, :] * (row_scale * total - goal) / island_tokens
        rbuf[step, own_rows(c), :] = result.astype(jnp.bfloat16)
        if paired:
            pair_r(step, 1, c).start()
            pair_r(step, 0, c).start()
        else:
            each(lambda k: r_copy(step, k, c).start())

    def forward(step, c):
        if paired:
            pair_r(step, 1, c).wait_recv()
            pair_r(step, 2, c).start()

    load_own.wait()
    for u in range(last_unit):
        if u % UNITS == UNITS - 1:
            vown[0, chunk_rows(u // UNITS), :] = take_unit(0, u)
        else:
            vacc[0] = take_unit(0, u)
        turn_unit(0, u)

    load_d.wait()
    each(lambda j: d_copy(j).wait_recv(), m)
    total_buf[slab_rows(isle), :] = lax.fori_loop(
        1, m, lambda j, total: total + dbuf[j], dbuf[0]
    )
    each(lambda j: a_copy(j).start(), m)

    load_tok.wait()

    def square(b, total):
        part = tok[:, pl.ds(pl.multiple_of(b * 128, 128), 128)].astype(jnp.float32)
        return total + part * part

    squares = lax.fori_loop(0, width // 128, square, jnp.zeros((rows, 128), jnp.float32))
    mean = jnp.sum(squares, axis=1, keepdims=True) / width
    scale[...] = lax.rsqrt(mean + NORM_EPSILON)
    keep_row = jnp.broadcast_to(mask[...].astype(jnp.float32), (128, rows))
    keep[...] = keep_row.T[:, :1]
    load_m1.wait()
    load_m2.wait()
    load_outer.wait()

    def outer_step():
        each(lambda j: a_copy(j).wait_recv(), m)
        each(lambda j: a_copy(j).wait_send(), m)

        def outer_block(b, carry):
            at = pl.ds(pl.multiple_of(b * BLOCK, BLOCK), BLOCK)
            outer_mean = total_buf[at, :] / m
            momentum_new = OUTER_MOMENTUM * outer_buf[at, :] + outer_mean
            momentum_out[at, :] = momentum_new
            update_out[at, :] = OUTER_RATE * (outer_mean + OUTER_MOMENTUM * momentum_new)
            return carry

        lax.fori_loop(0, blocks, outer_block, 0)

    for u in range(last_unit):
        c, q = u // UNITS, u % UNITS

        def arrive(k):
            x_copy(k, u).wait_recv()
            if u + WINDOW < last_unit:
                x_copy(k, u + WINDOW).start()
            vacc[k] = take_unit(k, u)
            if not paired and q == UNITS - 1:
                vsend[0, k - 1, chunk_rows(c), :] = vacc[k].astype(jnp.bfloat16)
                v_copy(0, k, c).start()
            if u < last_unit - 1:
                turn_unit(k, u)

        each(arrive)
        if paired and q == UNITS - 1:
            at = chunk_rows(c)
            for j, k in ((1, k_far), (0, k_partner)):
                vsend[0, j, at, :] = vacc[k].astype(jnp.bfloat16)
                pair_v(0, j, c).start()
            vcross[0, at, :] = vacc[2]
        if u == UNITS - 1:
            outer_step()
        for stage, act in enumerate((combine, residual, forward)):
            done = u - UNITS - stage
            if done >= 0 and done % UNITS == 0:
                act(0, done // UNITS)
    for stage, act in enumerate((combine, residual, forward)):
        for c in range(chunks):
            if UNITS * c + UNITS + stage >= last_unit:
                act(0, c)
        if stage == 0:
            each(lambda k: turn_unit(k, last_unit - 1))

    def update(step):
        for c in range(chunks):
            if paired:
                pair_r(step, 0, c).wait_recv()
                pair_r(step, 2, c).wait_recv()
            else:
                each(lambda k: r_copy(step, k, c).wait_recv())

        def gradient(b):
            at = pl.ds(pl.multiple_of(b * BLOCK, BLOCK), BLOCK)
            return jnp.dot(xt[at, :], rbuf[step], preferred_element_type=jnp.float32)

        gbuf[0] = gradient(0)

        def update_block(b, carry):
            at = pl.ds(pl.multiple_of(b * BLOCK, BLOCK), BLOCK)
            new_w, new_m1, new_m2 = adam_update(
                w[at, :], m1[at, :], m2[at, :], gbuf[b % 2], float(STEP_BASE + step + 1)
            )
            following = gradient(jnp.minimum(b + 1, blocks - 1))
            gbuf[(b + 1) % 2] = following
            if step == 0:
                w[at, :] = new_w
                m1[at, :] = new_m1
                m2[at, :] = new_m2
                wbf[at, :] = new_w.astype(jnp.bfloat16)
            else:
                out[at, :] = new_w
            return carry

        lax.fori_loop(0, blocks, update_block, 0)

    update(0)

    def partial(k):
        at = pl.ds(pl.multiple_of(source(k) * rows, CHUNK), rows)
        return jnp.dot(xbuf[at, :], wbf[...], preferred_element_type=jnp.float32)

    def send(k):
        vsend[1, k - 1] = partial(k).astype(jnp.bfloat16)
        for c in range(chunks):
            v_copy(1, k, c).start()

    if paired:
        for j, k in ((1, k_far), (0, k_partner)):
            vsend[1, j] = partial(k).astype(jnp.bfloat16)
            for c in range(chunks):
                pair_v(1, j, c).start()
        vcross[1] = partial(2)
    else:
        each(send)
    vown[1] = partial(0)
    for t in range(chunks + 2):
        for stage, act in enumerate((combine, residual, forward)):
            if 0 <= t - stage < chunks:
                act(1, t - stage)
    update(1)

    def drain(k):
        for u in range(last_unit):
            x_copy(k, u).wait_send()
        for c in range(chunks):
            for step in range(2):
                if not paired:
                    v_copy(step, k, c).wait_send()
                    r_copy(step, k, c).wait_send()

    each(drain)
    if paired:
        for step in range(2):
            for c in range(chunks):
                for j in range(3):
                    pair_v(step, j, c).wait_send()
                    pair_r(step, j, c).wait_send()
    each(lambda j: d_copy(j).wait_send(), m)


def train(n, m, tokens, targets, mask, gain, params, moment_one, moment_two, delta, momentum):
    rows, width = tokens.shape
    feat, columns = params.shape
    chunks = rows // CHUNK
    slab = delta.shape[0] // m
    vmem = pl.BlockSpec(memory_space=pltpu.VMEM)
    hbm = pl.BlockSpec(memory_space=pl.ANY)
    dma = pltpu.SemaphoreType.DMA
    bf16, f32 = jnp.bfloat16, jnp.float32
    return pl.pallas_call(
        functools.partial(inner_kernel, n, m),
        out_shape=(
            pltpu.VMEM((feat, columns), f32),
            pltpu.VMEM(momentum.shape, f32),
            pltpu.VMEM(momentum.shape, f32),
        ),
        in_specs=[hbm, vmem, vmem, vmem, hbm, hbm, hbm, hbm, hbm],
        out_specs=(vmem, vmem, vmem),
        scratch_shapes=[
            pltpu.VMEM((rows * n, feat), bf16),
            pltpu.VMEM((feat, rows * n), bf16),
            pltpu.VMEM((rows, width), bf16),
            pltpu.VMEM((feat, columns), f32),
            pltpu.VMEM((feat, columns), f32),
            pltpu.VMEM((feat, columns), f32),
            pltpu.VMEM((feat, columns), bf16),
            pltpu.VMEM((n, CHUNK, columns), f32),
            pltpu.VMEM((2, n - 1, rows, columns), bf16),
            pltpu.VMEM((2, n - 1, rows, columns), bf16),
            pltpu.VMEM((2, rows, columns), f32),
            pltpu.VMEM((2, rows, columns), f32),
            pltpu.VMEM((2, BLOCK, columns), f32),
            pltpu.VMEM((2, rows * n, columns), bf16),
            pltpu.VMEM((rows, 1), f32),
            pltpu.VMEM((rows, 1), f32),
            pltpu.VMEM((m, slab, delta.shape[1]), f32),
            pltpu.VMEM(delta.shape, f32),
            pltpu.VMEM(delta.shape, f32),
            dma((7,)),
            dma((n - 1, chunks * UNITS)),
            dma((n - 1, chunks * UNITS)),
            dma((2, n - 1, chunks)),
            dma((2, n - 1, chunks)),
            dma((2, n - 1, chunks)),
            dma((2, n - 1, chunks)),
            dma((m - 1,)),
            dma((m - 1,)),
            dma((m - 1,)),
            dma((m - 1,)),
        ],
        compiler_params=pltpu.CompilerParams(
            collective_id=0, has_side_effects=True, vmem_limit_bytes=54 * 2**20
        ),
        cost_estimate=pl.CostEstimate(
            flops=8 * rows * n * feat * columns,
            bytes_accessed=4 * rows * width + 16 * feat * columns,
            transcendentals=4 * feat * columns,
        ),
    )(tokens, targets, mask, gain, params, moment_one, moment_two, delta, momentum)


def per_device(
    tokens,
    targets,
    loss_mask,
    norm_gain,
    params,
    moment_one,
    moment_two,
    outer_delta,
    outer_momentum,
):
    weights, momentum_new, outer_update = train(
        lax.axis_size("fsdp"),
        lax.axis_size("island"),
        tokens[0],
        targets[0],
        loss_mask,
        norm_gain[None, :],
        params[0],
        moment_one[0],
        moment_two[0],
        outer_delta[0],
        outer_momentum,
    )
    return (weights[None], momentum_new, outer_update)


def solution(mesh):
    return jax.shard_map(
        per_device,
        mesh=mesh,
        in_specs=(
            P("island", "fsdp", None),
            P("island", "fsdp", None),
            P("island", "fsdp"),
            P(),
            P("island", "fsdp", None),
            P("island", "fsdp", None),
            P("island", "fsdp", None),
            P("island", "fsdp", None),
            P("fsdp", None),
        ),
        out_specs=(P("island", "fsdp", None), P("fsdp", None), P("fsdp", None)),
        check_vma=False,
    )
```

```python
import functools
import jax
import jax.numpy as jnp
from jax import lax
from jax.experimental import pallas as pl
from jax.experimental.pallas import tpu as pltpu
from jax.sharding import PartitionSpec as P

ADAM_BETA_ONE = 0.9
ADAM_BETA_TWO = 0.95
ADAM_EPSILON = 1e-08
INNER_RATE = 0.005
WEIGHT_DECAY = 0.1
NORM_EPSILON = 1e-05
OUTER_RATE = 0.7
OUTER_MOMENTUM = 0.9
STEP_BASE = 1000
MESH = pl.DeviceIdType.MESH
CHUNK = 64
BLOCK = 256
UNITS = 2
WINDOW = 3


def adam_update(weights, first_moment, second_moment, gradient, count):
    first_moment = ADAM_BETA_ONE * first_moment + (1.0 - ADAM_BETA_ONE) * gradient
    second_moment = ADAM_BETA_TWO * second_moment + (1.0 - ADAM_BETA_TWO) * gradient * gradient
    rate_one = INNER_RATE / (1.0 - ADAM_BETA_ONE**count)
    second_hat = second_moment * (1.0 / (1.0 - ADAM_BETA_TWO**count))
    weights = (1.0 - INNER_RATE * WEIGHT_DECAY) * weights - rate_one * first_moment / (
        second_hat * lax.rsqrt(second_hat) + ADAM_EPSILON
    )
    return (weights, first_moment, second_moment)


def inner_kernel(
    n,
    m,
    tokens,
    targets,
    mask,
    gain,
    params,
    moment_one,
    moment_two,
    delta,
    outer_momentum,
    out,
    momentum_out,
    update_out,
    xbuf,
    xt,
    tok,
    w,
    m1,
    m2,
    wbf,
    vacc,
    vsend,
    vrecv,
    vown,
    vcross,
    gbuf,
    rbuf,
    scale,
    keep,
    dbuf,
    total_buf,
    outer_buf,
    load_sem,
    x_send,
    x_recv,
    v_send,
    v_recv,
    r_send,
    r_recv,
    d_send,
    d_recv,
    a_send,
    a_recv,
):
    me = lax.axis_index("fsdp")
    isle = lax.axis_index("island")
    rows, width = tokens.shape
    feat = width // n
    chunks = rows // CHUNK
    blocks = feat // BLOCK
    unit = feat // UNITS
    island_tokens = rows * n
    slab = delta.shape[0] // m

    def peer(k):
        return lax.rem(me + k, n)

    def source(k):
        return lax.rem(me + n - k, n)

    def size(step):
        return CHUNK * (step + 1)

    def own_rows(c, step=0):
        return pl.ds(pl.multiple_of(me * rows + c * size(step), size(step)), size(step))

    def chunk_rows(c, step=0):
        return pl.ds(pl.multiple_of(c * size(step), size(step)), size(step))

    def slab_rows(i):
        return pl.ds(pl.multiple_of(i * slab, 8), slab)

    def x_copy(k, u):
        c, q = u // UNITS, u % UNITS
        to = peer(k)
        cols = pl.ds(pl.multiple_of(to * feat + q * unit, 128), unit)
        return pltpu.make_async_remote_copy(
            src_ref=tokens.at[chunk_rows(c), cols],
            dst_ref=xbuf.at[own_rows(c), pl.ds(q * unit, unit)],
            send_sem=x_send.at[k - 1, u],
            recv_sem=x_recv.at[k - 1, u],
            device_id={"fsdp": to},
            device_id_type=MESH,
        )

    def v_copy(step, k, c):
        return pltpu.make_async_remote_copy(
            src_ref=vsend.at[step, k - 1, chunk_rows(c, step)],
            dst_ref=vrecv.at[step, k - 1, chunk_rows(c, step)],
            send_sem=v_send.at[step, k - 1, c],
            recv_sem=v_recv.at[step, k - 1, c],
            device_id={"fsdp": source(k)},
            device_id_type=MESH,
        )

    def r_copy(step, k, c):
        return pltpu.make_async_remote_copy(
            src_ref=rbuf.at[step, own_rows(c, step)],
            dst_ref=rbuf.at[step, own_rows(c, step)],
            send_sem=r_send.at[step, k - 1, c],
            recv_sem=r_recv.at[step, k - 1, c],
            device_id={"fsdp": peer(k)},
            device_id_type=MESH,
        )

    paired = n == 4
    partner = me + 1 - 2 * lax.rem(me, 2)
    across = lax.rem(me + 2, 4)
    k_partner = 3 - 2 * lax.rem(me, 2)
    k_far = 4 - k_partner

    def pair_v(step, j, c):
        return pltpu.make_async_remote_copy(
            src_ref=vsend.at[step, j, chunk_rows(c, step)],
            dst_ref=vrecv.at[step, j, chunk_rows(c, step)],
            send_sem=v_send.at[step, j, c],
            recv_sem=v_recv.at[step, j, c],
            device_id={"fsdp": across if j == 2 else partner},
            device_id_type=MESH,
        )

    def pair_r(step, j, c):
        owner = across if j == 2 else me
        first = pl.multiple_of(owner * rows + c * size(step), size(step))
        at = pl.ds(first, size(step))
        return pltpu.make_async_remote_copy(
            src_ref=rbuf.at[step, at],
            dst_ref=rbuf.at[step, at],
            send_sem=r_send.at[step, j, c],
            recv_sem=r_recv.at[step, j, c],
            device_id={"fsdp": across if j == 1 else partner},
            device_id_type=MESH,
        )

    def d_copy(j):
        to = lax.rem(isle + j, m)
        return pltpu.make_async_remote_copy(
            src_ref=delta.at[slab_rows(to)],
            dst_ref=dbuf.at[j],
            send_sem=d_send.at[j - 1],
            recv_sem=d_recv.at[j - 1],
            device_id={"island": to},
            device_id_type=MESH,
        )

    def a_copy(j):
        return pltpu.make_async_remote_copy(
            src_ref=total_buf.at[slab_rows(isle)],
            dst_ref=total_buf.at[slab_rows(isle)],
            send_sem=a_send.at[j - 1],
            recv_sem=a_recv.at[j - 1],
            device_id={"island": lax.rem(isle + j, m)},
            device_id_type=MESH,
        )

    def each(body, count=n):
        def run(k, carry):
            body(k)
            return carry

        lax.fori_loop(1, count, run, 0)

    barrier = pltpu.get_barrier_semaphore()
    each(
        lambda k: pl.semaphore_signal(
            barrier, inc=1, device_id={"fsdp": peer(k)}, device_id_type=MESH
        )
    )
    each(
        lambda j: pl.semaphore_signal(
            barrier, inc=1, device_id={"island": lax.rem(isle + j, m)}, device_id_type=MESH
        ),
        m,
    )
    pl.semaphore_wait(barrier, n + m - 2)

    last_unit = chunks * UNITS
    for u in range(min(WINDOW, last_unit)):
        each(lambda k: x_copy(k, u).start())

    load_own = pltpu.make_async_copy(
        tokens.at[:, pl.ds(pl.multiple_of(me * feat, 128), feat)],
        xbuf.at[pl.ds(pl.multiple_of(me * rows, CHUNK), rows)],
        load_sem.at[0],
    )
    load_w = pltpu.make_async_copy(params, w, load_sem.at[1])
    load_tok = pltpu.make_async_copy(tokens, tok, load_sem.at[2])
    load_m1 = pltpu.make_async_copy(moment_one, m1, load_sem.at[3])
    load_m2 = pltpu.make_async_copy(moment_two, m2, load_sem.at[4])
    load_d = pltpu.make_async_copy(delta.at[slab_rows(isle)], dbuf.at[0], load_sem.at[5])
    load_outer = pltpu.make_async_copy(outer_momentum, outer_buf, load_sem.at[6])
    load_w.start()
    load_own.start()
    each(lambda j: d_copy(j).start(), m)
    for load in (load_d, load_tok, load_m1, load_m2, load_outer):
        load.start()

    load_w.wait()

    def cast_block(b, carry):
        at = pl.ds(pl.multiple_of(b * BLOCK, BLOCK), BLOCK)
        wbf[at, :] = w[at, :].astype(jnp.bfloat16)
        return carry

    lax.fori_loop(0, blocks, cast_block, 0)

    def take_unit(k, u):
        c, q = u // UNITS, u % UNITS
        at = pl.ds(pl.multiple_of(source(k) * rows + c * CHUNK, CHUNK), CHUNK)
        for b in range(unit // 128):
            first = q * unit + b * 128
            cols = pl.ds(first, 128)
            gains = gain[:, pl.ds(pl.multiple_of(me * feat + first, 128), 128)]
            scaled = xbuf[at, cols].astype(jnp.float32) * gains
            xbuf[at, cols] = scaled.astype(jnp.bfloat16)
        cols = pl.ds(q * unit, unit)
        part = jnp.dot(xbuf[at, cols], wbf[cols, :], preferred_element_type=jnp.float32)
        return part if q == 0 else vacc[k] + part

    def turn_unit(k, u):
        c, q = u // UNITS, u % UNITS
        if c % 2:
            start = source(k) * rows + (c - 1) * CHUNK
            at = pl.ds(pl.multiple_of(start, 2 * CHUNK), 2 * CHUNK)
            for b in range(unit // 128):
                cols = pl.ds(q * unit + b * 128, 128)
                xt[cols, at] = xbuf[at, cols].astype(jnp.float32).T.astype(jnp.bfloat16)

    def combine(step, c):
        if paired:
            at = chunk_rows(c, step)
            pair_v(step, 1, c).wait_recv()
            both = vcross[step, at, :] + vrecv[step, 1, at, :].astype(jnp.float32)
            vsend[step, 2, at, :] = both.astype(jnp.bfloat16)
            pair_v(step, 2, c).start()

    def residual(step, c):
        at = chunk_rows(c, step)
        total = vown[step, at, :]
        if paired:
            for j in (0, 2):
                pair_v(step, j, c).wait_recv()
                total = total + vrecv[step, j, at, :].astype(jnp.float32)
        else:
            each(lambda k: v_copy(step, k, c).wait_recv())
            for k in range(1, n):
                total = total + vrecv[step, k - 1, at, :].astype(jnp.float32)
        row_scale = scale[at, :]
        goal = targets[at, :].astype(jnp.float32)
        result = row_scale * keep[at, :] * (row_scale * total - goal) / island_tokens
        rbuf[step, own_rows(c, step), :] = result.astype(jnp.bfloat16)
        if paired:
            pair_r(step, 1, c).start()
            pair_r(step, 0, c).start()
        else:
            each(lambda k: r_copy(step, k, c).start())

    def forward(step, c):
        if paired:
            pair_r(step, 1, c).wait_recv()
            pair_r(step, 2, c).start()

    load_own.wait()
    for u in range(last_unit):
        if u % UNITS == UNITS - 1:
            vown[0, chunk_rows(u // UNITS), :] = take_unit(0, u)
        else:
            vacc[0] = take_unit(0, u)
        turn_unit(0, u)

    load_d.wait()
    each(lambda j: d_copy(j).wait_recv(), m)
    total_buf[slab_rows(isle), :] = lax.fori_loop(
        1, m, lambda j, total: total + dbuf[j], dbuf[0]
    )
    each(lambda j: a_copy(j).start(), m)

    load_tok.wait()

    def square(b, total):
        part = tok[:, pl.ds(pl.multiple_of(b * 128, 128), 128)].astype(jnp.float32)
        return total + part * part

    squares = lax.fori_loop(0, width // 128, square, jnp.zeros((rows, 128), jnp.float32))
    mean = jnp.sum(squares, axis=1, keepdims=True) / width
    scale[...] = lax.rsqrt(mean + NORM_EPSILON)
    keep_row = jnp.broadcast_to(mask[...].astype(jnp.float32), (128, rows))
    keep[...] = keep_row.T[:, :1]
    load_m1.wait()
    load_m2.wait()
    load_outer.wait()

    def outer_step():
        each(lambda j: a_copy(j).wait_recv(), m)
        each(lambda j: a_copy(j).wait_send(), m)

        def outer_block(b, carry):
            at = pl.ds(pl.multiple_of(b * BLOCK, BLOCK), BLOCK)
            outer_mean = total_buf[at, :] / m
            momentum_new = OUTER_MOMENTUM * outer_buf[at, :] + outer_mean
            momentum_out[at, :] = momentum_new
            update_out[at, :] = OUTER_RATE * (outer_mean + OUTER_MOMENTUM * momentum_new)
            return carry

        lax.fori_loop(0, blocks, outer_block, 0)

    for u in range(last_unit):
        c, q = u // UNITS, u % UNITS

        def arrive(k):
            x_copy(k, u).wait_recv()
            if u + WINDOW < last_unit:
                x_copy(k, u + WINDOW).start()
            vacc[k] = take_unit(k, u)
            if not paired and q == UNITS - 1:
                vsend[0, k - 1, chunk_rows(c), :] = vacc[k].astype(jnp.bfloat16)
                v_copy(0, k, c).start()
            if u < last_unit - 1:
                turn_unit(k, u)

        each(arrive)
        if paired and q == UNITS - 1:
            at = chunk_rows(c)
            for j, k in ((1, k_far), (0, k_partner)):
                vsend[0, j, at, :] = vacc[k].astype(jnp.bfloat16)
                pair_v(0, j, c).start()
            vcross[0, at, :] = vacc[2]
        if u == UNITS - 1:
            outer_step()
        for stage, act in enumerate((combine, residual, forward)):
            done = u - UNITS - stage
            if done >= 0 and done % UNITS == 0:
                act(0, done // UNITS)
    for stage, act in enumerate((combine, residual, forward)):
        for c in range(chunks):
            if UNITS * c + UNITS + stage >= last_unit:
                act(0, c)
        if stage == 0:
            each(lambda k: turn_unit(k, last_unit - 1))

    def update(step):
        for c in range(chunks // (step + 1)):
            if paired:
                pair_r(step, 0, c).wait_recv()
                pair_r(step, 2, c).wait_recv()
            else:
                each(lambda k: r_copy(step, k, c).wait_recv())

        def gradient(b):
            at = pl.ds(pl.multiple_of(b * BLOCK, BLOCK), BLOCK)
            return jnp.dot(xt[at, :], rbuf[step], preferred_element_type=jnp.float32)

        gbuf[0] = gradient(0)

        def update_block(b, carry):
            at = pl.ds(pl.multiple_of(b * BLOCK, BLOCK), BLOCK)
            new_w, new_m1, new_m2 = adam_update(
                w[at, :], m1[at, :], m2[at, :], gbuf[b % 2], float(STEP_BASE + step + 1)
            )
            following = gradient(jnp.minimum(b + 1, blocks - 1))
            gbuf[(b + 1) % 2] = following
            if step == 0:
                w[at, :] = new_w
                m1[at, :] = new_m1
                m2[at, :] = new_m2
                wbf[at, :] = new_w.astype(jnp.bfloat16)
            else:
                out[at, :] = new_w
            return carry

        lax.fori_loop(0, blocks, update_block, 0)

    update(0)

    def partial(k):
        at = pl.ds(pl.multiple_of(source(k) * rows, CHUNK), rows)
        return jnp.dot(xbuf[at, :], wbf[...], preferred_element_type=jnp.float32)

    def send(k):
        vsend[1, k - 1] = partial(k).astype(jnp.bfloat16)
        for c in range(chunks // 2):
            v_copy(1, k, c).start()

    if paired:
        for j, k in ((1, k_far), (0, k_partner)):
            vsend[1, j] = partial(k).astype(jnp.bfloat16)
            for c in range(chunks // 2):
                pair_v(1, j, c).start()
        vcross[1] = partial(2)
    else:
        each(send)
    vown[1] = partial(0)
    for t in range(chunks // 2 + 2):
        for stage, act in enumerate((combine, residual, forward)):
            if 0 <= t - stage < chunks // 2:
                act(1, t - stage)
    update(1)

    def drain(k):
        for u in range(last_unit):
            x_copy(k, u).wait_send()
        for step in range(2):
            for c in range(chunks // (step + 1)):
                if not paired:
                    v_copy(step, k, c).wait_send()
                    r_copy(step, k, c).wait_send()

    each(drain)
    if paired:
        for step in range(2):
            for c in range(chunks // (step + 1)):
                for j in range(3):
                    pair_v(step, j, c).wait_send()
                    pair_r(step, j, c).wait_send()
    each(lambda j: d_copy(j).wait_send(), m)


def train(n, m, tokens, targets, mask, gain, params, moment_one, moment_two, delta, momentum):
    rows, width = tokens.shape
    feat, columns = params.shape
    chunks = rows // CHUNK
    slab = delta.shape[0] // m
    vmem = pl.BlockSpec(memory_space=pltpu.VMEM)
    hbm = pl.BlockSpec(memory_space=pl.ANY)
    dma = pltpu.SemaphoreType.DMA
    bf16, f32 = jnp.bfloat16, jnp.float32
    return pl.pallas_call(
        functools.partial(inner_kernel, n, m),
        out_shape=(
            pltpu.VMEM((feat, columns), f32),
            pltpu.VMEM(momentum.shape, f32),
            pltpu.VMEM(momentum.shape, f32),
        ),
        in_specs=[hbm, vmem, vmem, vmem, hbm, hbm, hbm, hbm, hbm],
        out_specs=(vmem, vmem, vmem),
        scratch_shapes=[
            pltpu.VMEM((rows * n, feat), bf16),
            pltpu.VMEM((feat, rows * n), bf16),
            pltpu.VMEM((rows, width), bf16),
            pltpu.VMEM((feat, columns), f32),
            pltpu.VMEM((feat, columns), f32),
            pltpu.VMEM((feat, columns), f32),
            pltpu.VMEM((feat, columns), bf16),
            pltpu.VMEM((n, CHUNK, columns), f32),
            pltpu.VMEM((2, n - 1, rows, columns), bf16),
            pltpu.VMEM((2, n - 1, rows, columns), bf16),
            pltpu.VMEM((2, rows, columns), f32),
            pltpu.VMEM((2, rows, columns), f32),
            pltpu.VMEM((2, BLOCK, columns), f32),
            pltpu.VMEM((2, rows * n, columns), bf16),
            pltpu.VMEM((rows, 1), f32),
            pltpu.VMEM((rows, 1), f32),
            pltpu.VMEM((m, slab, delta.shape[1]), f32),
            pltpu.VMEM(delta.shape, f32),
            pltpu.VMEM(delta.shape, f32),
            dma((7,)),
            dma((n - 1, chunks * UNITS)),
            dma((n - 1, chunks * UNITS)),
            dma((2, n - 1, chunks)),
            dma((2, n - 1, chunks)),
            dma((2, n - 1, chunks)),
            dma((2, n - 1, chunks)),
            dma((m - 1,)),
            dma((m - 1,)),
            dma((m - 1,)),
            dma((m - 1,)),
        ],
        compiler_params=pltpu.CompilerParams(
            collective_id=0, has_side_effects=True, vmem_limit_bytes=54 * 2**20
        ),
        cost_estimate=pl.CostEstimate(
            flops=8 * rows * n * feat * columns,
            bytes_accessed=4 * rows * width + 16 * feat * columns,
            transcendentals=4 * feat * columns,
        ),
    )(tokens, targets, mask, gain, params, moment_one, moment_two, delta, momentum)


def per_device(
    tokens,
    targets,
    loss_mask,
    norm_gain,
    params,
    moment_one,
    moment_two,
    outer_delta,
    outer_momentum,
):
    weights, momentum_new, outer_update = train(
        lax.axis_size("fsdp"),
        lax.axis_size("island"),
        tokens[0],
        targets[0],
        loss_mask,
        norm_gain[None, :],
        params[0],
        moment_one[0],
        moment_two[0],
        outer_delta[0],
        outer_momentum,
    )
    return (weights[None], momentum_new, outer_update)


def solution(mesh):
    return jax.shard_map(
        per_device,
        mesh=mesh,
        in_specs=(
            P("island", "fsdp", None),
            P("island", "fsdp", None),
            P("island", "fsdp"),
            P(),
            P("island", "fsdp", None),
            P("island", "fsdp", None),
            P("island", "fsdp", None),
            P("island", "fsdp", None),
            P("fsdp", None),
        ),
        out_specs=(P("island", "fsdp", None), P("fsdp", None), P("fsdp", None)),
        check_vma=False,
    )
```
